32 devices in a mesh: row: 4 (over y, x), col: 8 (over z, core).
Axes of the slice: x: 2, y: 2, z: 4, core: 2. Of those that a mesh axis runs over, the one named last changes fastest.
Arguments:
- user_emb: bfloat16 [8192, 256], P(('row', 'col')), may hold values from -8 to 8
- item_emb: bfloat16 [8192, 256], P(('row', 'col')), may hold values from -8 to 8
- user_cot: bfloat16 [8192, 256], P(('row', 'col')), may hold values from -8 to 8
- item_cot: bfloat16 [8192, 256], P(('row', 'col')), may hold values from -8 to 8
- tiles: bfloat16 [8192, 5120], P('row', 'col'), may hold values from 0 to 1, as said below
- tile_cols: int32 [64, 40], P('row', 'col'), may hold values from 0 to 7, as said below
- row_count: int32 [64, 8], P('row', 'col'), may hold values from 1 to 5, as said below
- user_deg: int32 [8192], P(('row', 'col')), may hold values from 6 to 21
- item_deg: int32 [8192], P(('row', 'col')), may hold values from 6 to 21
Outputs:
- user_next: float32 [8192, 256], P(('row', 'col'))
- item_next: float32 [8192, 256], P(('row', 'col'))
- user_grad: float32 [8192, 256], P(('row', 'col'))
- item_grad: float32 [8192, 256], P(('row', 'col'))
The draws below stay inside these ranges and needn't reach their ends.
Inputs may be any that keep to these rules, and one draw needn't show every extreme that they name: `tiles`: every entry is 0 or 1. `tile_cols`: within one block row of one device, the 5 slots name distinct item blocks; slots at or beyond row_count are unused. `row_count`: in every draw some block row of some device holds 5 tiles.
All inputs are finite; a program needn't handle non-finite values.
Results may differ from the reference program's by a relative error of at most 0.0029.
Values may be sent and summed in bfloat16 or wider, within the bound.
No kernel may reach another device: no remote copies, remote signals or barrier semaphores. Data moves between devices by JAX's collectives and lax.ppermute only.
A program may use at most 128 MiB of HBM per device.

```python
import jax
import jax.numpy as jnp
from jax import lax

FEAT = 256
BLK = 128
UD = 256
ID = 256
GRID_ROWS = 4
GRID_COLS = 8
USERS = 8192
ITEMS = 8192
UBLK = 16
IBLK = 8
KR = 5
N_ROW = 4
N_COL = 8


def node_features(key, salt, count):
    salted = jax.random.fold_in(key, salt)
    values = jax.random.normal(jax.random.fold_in(salted, 2), (count, FEAT), jnp.float32)
    return jnp.clip(values, -8.0, 8.0).astype(jnp.bfloat16)


def draw_user_emb(key, part):
    return node_features(key, 11, USERS)


def draw_item_emb(key, part):
    return node_features(key, 12, ITEMS)


def draw_user_cot(key, part):
    return node_features(key, 13, USERS)


def draw_item_cot(key, part):
    return node_features(key, 14, ITEMS)


def draw_tiles(key, part):
    tile_rows = N_ROW * UBLK
    tile_slots = N_COL * KR
    levels = jax.random.randint(jax.random.fold_in(key, 31), (tile_rows, 1, tile_slots, 1), 2, 9)
    coin_flip = jax.random.randint(jax.random.fold_in(key, 32), (tile_rows, BLK, tile_slots, BLK), 0, 16)
    filled = (coin_flip < levels).astype(jnp.float32)
    return filled.reshape(tile_rows * BLK, tile_slots * BLK).astype(jnp.bfloat16)


def draw_tile_cols(key, part):
    scores = jax.random.randint(jax.random.fold_in(key, 51), (N_ROW * UBLK, N_COL, IBLK), 0, 65536)
    scores = scores * IBLK + jnp.arange(IBLK, dtype=jnp.int32)
    ranked = jnp.argsort(scores, axis=-1, stable=True).astype(jnp.int32)
    return ranked[:, :, :KR].reshape(N_ROW * UBLK, N_COL * KR)


def draw_row_count(key, part):
    heavy_device = jax.random.randint(jax.random.fold_in(key, 41), (N_ROW, 1, N_COL), 0, 4)
    weight = jnp.where(heavy_device == 3, 4, 1)
    uniform_part = jax.random.randint(jax.random.fold_in(key, 42), (N_ROW, UBLK, N_COL), 0, KR)
    counts = jnp.minimum(KR, 1 + uniform_part * weight // 4)
    special = jax.random.randint(jax.random.fold_in(key, 43), (), 0, N_ROW * UBLK * N_COL)
    places = jnp.arange(N_ROW * UBLK * N_COL, dtype=jnp.int32).reshape(N_ROW, UBLK, N_COL)
    counts = jnp.where(places == special, KR, counts)
    return counts.reshape(N_ROW * UBLK, N_COL).astype(jnp.int32)


def touch_ends(array, stream_key, low, top_value):
    extent = array.shape
    spot = [jax.random.randint(jax.random.fold_in(stream_key, axis), (), 0, extent[axis]) for axis in range(len(extent))]
    array = array.at[tuple(spot)].set(low)
    longest = extent.index(max(extent))
    spot[longest] = (spot[longest] + 1) % extent[longest]
    return array.at[tuple(spot)].set(top_value)


def setup_inputs(seed: int = 0) -> dict:
    arg_keys = jax.random.split(jax.random.key(seed), 10)
    user_emb = draw_user_emb(jax.random.fold_in(arg_keys[9], 71), 0)
    item_emb = draw_item_emb(jax.random.fold_in(arg_keys[9], 71), 0)
    user_cot = draw_user_cot(jax.random.fold_in(arg_keys[9], 71), 0)
    item_cot = draw_item_cot(jax.random.fold_in(arg_keys[9], 71), 0)
    tiles = draw_tiles(jax.random.fold_in(arg_keys[9], 71), 0)
    tile_cols = draw_tile_cols(jax.random.fold_in(arg_keys[9], 71), 0)
    row_count = draw_row_count(jax.random.fold_in(arg_keys[9], 71), 0)
    user_deg = touch_ends(jax.random.randint(arg_keys[7], (USERS,), GRID_COLS * KR * BLK // 1024 + 1, GRID_COLS * KR * BLK // 256 + 2), jax.random.fold_in(arg_keys[7], 1), GRID_COLS * KR * BLK // 1024 + 1, (GRID_COLS * KR * BLK // 256 + 2) - 1).astype(jnp.int32)
    item_deg = touch_ends(jax.random.randint(arg_keys[8], (ITEMS,), GRID_ROWS * UBLK * KR * BLK // (1024 * IBLK) + 1, GRID_ROWS * UBLK * KR * BLK // (256 * IBLK) + 2), jax.random.fold_in(arg_keys[8], 1), GRID_ROWS * UBLK * KR * BLK // (1024 * IBLK) + 1, (GRID_ROWS * UBLK * KR * BLK // (256 * IBLK) + 2) - 1).astype(jnp.int32)
    return {"user_emb": user_emb, "item_emb": item_emb, "user_cot": user_cot, "item_cot": item_cot, "tiles": tiles, "tile_cols": tile_cols, "row_count": row_count, "user_deg": user_deg, "item_deg": item_deg}


def scaled_side(former, latter, inverse_root):
    joined = jnp.concatenate([former, latter], axis=1).astype(jnp.float32)
    return (joined * inverse_root[:, None]).astype(jnp.bfloat16)

def reference(user_emb, item_emb, user_cot, item_cot, tiles, tile_cols, row_count, user_deg, item_deg):
    doubled = 2 * FEAT
    panel_users = N_COL * UD
    user_root = 1.0 / jnp.sqrt(user_deg.astype(jnp.float32))
    item_root = 1.0 / jnp.sqrt(item_deg.astype(jnp.float32))
    user_side = scaled_side(user_emb, user_cot, user_root)
    item_side = scaled_side(item_emb, item_cot, item_root)
    item_grid = item_side.reshape(N_ROW, N_COL, ID, doubled)

    def visit_device(device_id, totals):
        user_total, item_total = totals
        grid_row = (device_id // N_COL).astype(jnp.int32)
        grid_col = (device_id % N_COL).astype(jnp.int32)
        tile_part = lax.dynamic_slice(tiles, (grid_row * (UBLK * BLK), grid_col * (KR * BLK)), (UBLK * BLK, KR * BLK))
        col_ids = lax.dynamic_slice(tile_cols, (grid_row * UBLK, grid_col * KR), (UBLK, KR)).astype(jnp.int32)
        counts = lax.dynamic_slice(row_count, (grid_row * UBLK, grid_col), (UBLK, 1))
        live_mask = (jnp.arange(KR, dtype=jnp.int32)[None, :] < counts).astype(jnp.float32)
        tile_grid = tile_part.reshape(UBLK, BLK, KR, BLK).astype(jnp.float32) * live_mask[:, None, :, None]
        item_panel = lax.dynamic_slice_in_dim(item_grid, grid_col, 1, 1).reshape(IBLK, BLK, doubled).astype(jnp.float32)
        user_panel = lax.dynamic_slice_in_dim(user_side, grid_row * panel_users, panel_users, 0).reshape(UBLK, BLK, doubled).astype(jnp.float32)
        user_part = jnp.einsum('bikj,bkjf->bif', tile_grid, item_panel[col_ids])
        item_terms = jnp.einsum('bikj,bif->bkjf', tile_grid, user_panel).reshape(UBLK * KR, BLK, doubled)
        item_part = jax.ops.segment_sum(item_terms, col_ids.reshape(-1), num_segments=IBLK)
        old_users = lax.dynamic_slice_in_dim(user_total, grid_row * panel_users, panel_users, 0)
        user_total = lax.dynamic_update_slice_in_dim(user_total, old_users + user_part.reshape(panel_users, doubled), grid_row * panel_users, 0)
        old_items = lax.dynamic_slice_in_dim(item_total, grid_col, 1, 1)
        item_total = lax.dynamic_update_slice_in_dim(item_total, old_items + item_part.reshape(N_ROW, 1, ID, doubled), grid_col, 1)
        return (user_total, item_total)
    start_users = jnp.zeros((USERS, doubled), jnp.float32)
    start_items = jnp.zeros((N_ROW, N_COL, ID, doubled), jnp.float32)
    user_total, item_total = lax.fori_loop(0, N_ROW * N_COL, visit_device, (start_users, start_items))
    item_total = item_total.reshape(ITEMS, doubled)
    user_out = user_total * user_root[:, None]
    item_out = item_total * item_root[:, None]
    return (user_out[:, :FEAT], item_out[:, :FEAT], user_out[:, FEAT:], item_out[:, FEAT:])
```

```python
import functools

import jax
import jax.numpy as jnp
from jax import lax
from jax.experimental import pallas as pl
from jax.experimental.pallas import tpu as pltpu
from jax.sharding import PartitionSpec as P

VMEM_BYTES = 40 * 1024 * 1024


def swap(value, axis, count, mask):
    return lax.ppermute(value, axis, [(i, i ^ mask) for i in range(count)])


def full(shape):
    return pl.BlockSpec(shape, lambda *_: (0,) * len(shape))


def params():
    return pltpu.CompilerParams(vmem_limit_bytes=VMEM_BYTES)


def cost(rows, depth, columns):
    return pl.CostEstimate(
        flops=2 * rows * depth * columns,
        bytes_accessed=2 * (rows * depth + depth * columns + rows * columns),
        transcendentals=0,
    )


def dense_kernel(block, slots, order, cols, counts, place, tiles_ref, dense_ref, turned_ref):
    dense_ref[...] = jnp.zeros_like(dense_ref)
    turned_ref[...] = jnp.zeros_like(turned_ref)
    row = order[pl.program_id(0)]
    for k in range(slots):

        @pl.when(k < counts[row, 0])
        def _():
            at = pl.multiple_of(place[cols[row, k]] * block, block)
            tile = tiles_ref[:, k * block : (k + 1) * block]
            dense_ref[:, pl.ds(at, block)] = tile
            turned_ref[pl.ds(at, block), :] = tile.T


def densify(tiles, tile_cols, row_count, order, place, item_blocks):
    block_rows, slots = tile_cols.shape
    block = tiles.shape[0] // block_rows
    items = item_blocks * block
    grid_spec = pltpu.PrefetchScalarGridSpec(
        num_scalar_prefetch=4,
        grid=(block_rows,),
        in_specs=[pl.BlockSpec((block, slots * block), lambda b, order, *_: (order[b], 0))],
        out_specs=[
            pl.BlockSpec((block, items), lambda b, *_: (b, 0)),
            pl.BlockSpec((items, block), lambda b, *_: (0, b)),
        ],
    )
    return pl.pallas_call(
        functools.partial(dense_kernel, block, slots),
        grid_spec=grid_spec,
        out_shape=[
            jax.ShapeDtypeStruct((block_rows * block, items), tiles.dtype),
            jax.ShapeDtypeStruct((items, block_rows * block), tiles.dtype),
        ],
        compiler_params=params(),
        name="densify",
    )(order, tile_cols, row_count, place, tiles)


def gather_scratch(parts, whole):
    rows = parts[0].shape[0]
    for i, part in enumerate(parts):
        whole[i * rows : (i + 1) * rows, :] = part[...]


def products(matrix, row_of, parts, added=None):
    rows, width = parts[0].shape
    depth = len(parts) * rows
    steps = len(row_of)
    stride = row_of[1] - row_of[0] if steps > 1 else 1
    base = row_of[0]
    count = len(parts)

    def kernel(*refs):
        matrix_ref, part_refs = refs[0], refs[1 : 1 + count]
        rest = refs[1 + count :]
        if added is not None:
            added_ref, rest = rest[0], rest[1:]
        outs, whole = rest[:steps], rest[steps]
        step = pl.program_id(0)

        @pl.when(step == 0)
        def _():
            gather_scratch(part_refs, whole)

        total = jnp.dot(matrix_ref[...], whole[...], preferred_element_type=jnp.float32)
        if added is not None:
            total = total + added_ref[...].astype(jnp.float32)
        for s, out in enumerate(outs):

            @pl.when(step == s)
            def _(out=out):
                out[...] = total.astype(out.dtype)

    in_specs = [pl.BlockSpec((rows, depth), lambda s: (base + stride * s, 0))]
    in_specs += [full((rows, width))] * count
    operands = [matrix, *parts]
    if added is not None:
        in_specs.append(pl.BlockSpec((rows, width), lambda s: (s, 0)))
        operands.append(added)
    kinds = [jnp.float32 if s == 0 else jnp.bfloat16 for s in range(steps)]
    return pl.pallas_call(
        kernel,
        grid=(steps,),
        in_specs=in_specs,
        out_specs=[full((rows, width))] * steps,
        out_shape=[jax.ShapeDtypeStruct((rows, width), kind) for kind in kinds],
        scratch_shapes=[pltpu.VMEM((depth, width), jnp.bfloat16)],
        compiler_params=params(),
        cost_estimate=cost(steps * rows, depth, width),
        name="products",
    )(*operands)


def stacked_products(matrix, row_of, parts):
    rows, width = parts[0].shape
    depth = len(parts) * rows
    steps = len(row_of)
    stride = row_of[1] - row_of[0] if steps > 1 else 1
    base = row_of[0]
    count = len(parts)

    def kernel(*refs):
        matrix_ref, part_refs, out, whole = refs[0], refs[1 : 1 + count], refs[1 + count], refs[2 + count]

        @pl.when(pl.program_id(0) == 0)
        def _():
            gather_scratch(part_refs, whole)

        out[...] = jnp.dot(matrix_ref[...], whole[...], preferred_element_type=jnp.float32).astype(out.dtype)

    return pl.pallas_call(
        kernel,
        grid=(steps,),
        in_specs=[pl.BlockSpec((rows, depth), lambda s: (base + stride * s, 0))] + [full((rows, width))] * count,
        out_specs=pl.BlockSpec((rows, width), lambda s: (s, 0)),
        out_shape=jax.ShapeDtypeStruct((steps * rows, width), jnp.bfloat16),
        scratch_shapes=[pltpu.VMEM((depth, width), jnp.bfloat16)],
        compiler_params=params(),
        cost_estimate=cost(steps * rows, depth, width),
        name="stacked_products",
    )(matrix, *parts)


def finish(own, others, root):
    rows, width = own.shape

    def kernel(*refs):
        own_ref, root_ref, other_refs, (left, right) = refs[0], refs[1], refs[2:-2], refs[-2:]
        total = own_ref[...]
        for other in other_refs:
            total = total + other[...].astype(jnp.float32)
        total = total * root_ref[...]
        left[...] = total[:, : width // 2]
        right[...] = total[:, width // 2 :]

    return pl.pallas_call(
        kernel,
        out_shape=[jax.ShapeDtypeStruct((rows, width // 2), jnp.float32)] * 2,
        compiler_params=params(),
        cost_estimate=pl.CostEstimate(
            flops=rows * width * (len(others) + 1), bytes_accessed=rows * width * (8 + 2 * len(others)), transcendentals=0
        ),
        name="finish",
    )(own, root, *others)


def scaled_side(former, latter, root):
    joined = jnp.concatenate([former, latter], axis=1).astype(jnp.float32)
    return (joined * root).astype(jnp.bfloat16)


def shards(n_row, n_col, user_emb, item_emb, user_cot, item_cot, tiles, tile_cols, row_count, user_deg, item_deg):
    block_rows, slots = tile_cols.shape
    block = tiles.shape[0] // block_rows
    here_row, here_col = lax.axis_index("row"), lax.axis_index("col")
    item_rows = item_emb.shape[0]
    user_rows = user_emb.shape[0]
    item_blocks = n_row * item_rows // block
    per_item, per_user = item_rows // block, user_rows // block

    user_root = 1.0 / jnp.sqrt(user_deg.astype(jnp.float32))[:, None]
    item_root = 1.0 / jnp.sqrt(item_deg.astype(jnp.float32))[:, None]
    item_side = scaled_side(item_emb, item_cot, item_root)
    user_side = scaled_side(user_emb, user_cot, user_root)

    item_parts = [item_side] + [swap(item_side, "row", n_row, k) for k in range(1, n_row)]
    user_even = [user_side] + [swap(user_side, "col", n_col, 2 * j) for j in range(1, n_col // 2)]
    user_parts = []
    for part in user_even:
        user_parts += [part, swap(part, "col", n_col, 1)]

    block_ids = jnp.arange(block_rows, dtype=jnp.int32)
    order = ((block_ids // per_user) ^ here_col) * per_user + block_ids % per_user
    item_ids = jnp.arange(item_blocks, dtype=jnp.int32)
    place = ((item_ids // per_item) ^ here_row) * per_item + item_ids % per_item
    dense, turned = densify(tiles, tile_cols, row_count, order, place, item_blocks)

    to_sibling = stacked_products(dense, list(range(1, n_col, 2)), item_parts)
    from_sibling = swap(to_sibling, "col", n_col, 1)
    user_sums = products(dense, list(range(0, n_col, 2)), item_parts, from_sibling)
    user_others = [swap(user_sums[j], "col", n_col, 2 * j) for j in range(1, n_col // 2)]

    item_sums = products(turned, list(range(n_row)), user_parts)
    item_others = [swap(item_sums[k], "row", n_row, k) for k in range(1, n_row)]

    user_next, user_grad = finish(user_sums[0], user_others, user_root)
    item_next, item_grad = finish(item_sums[0], item_others, item_root)
    return (user_next, item_next, user_grad, item_grad)


def solution(mesh):
    nodes = P(("row", "col"), None)
    in_specs = (nodes,) * 4 + (P("row", "col"),) * 3 + (P(("row", "col")),) * 2
    body = functools.partial(shards, mesh.shape["row"], mesh.shape["col"])
    return jax.shard_map(body, mesh=mesh, in_specs=in_specs, out_specs=(nodes,) * 4, check_vma=False)
```
